256 devices in a mesh: ctx: 64 (over x, y, z_lo, core), ch: 4 (over z_hi).
Axes of the slice: x: 4, y: 4, z: 8 (z_hi: 4, z_lo: 2; z = z_hi * 2 + z_lo), core: 2. Of those that a mesh axis runs over, the one named last changes fastest.
Arguments:
- tokens: bfloat16 [8192, 8192], P('ctx', 'ch'), may hold values from -6 to 6
- value_weight: bfloat16 [8192, 2048], P('ctx', 'ch'), may hold values from -0.0625 to 0.0625
- gate_stream: bfloat16 [8192, 2048], P('ctx', 'ch'), may hold values from -6 to 6
- decay_rate: float32 [16, 2048], P(None, 'ch'), may hold values from 0.5 to 800
- frequency: float32 [16, 2048], P(None, 'ch'), may hold values from 0 to 0.2
- residue: float32 [16, 2048], P(None, 'ch'), may hold values from -2.5 to 2.5
- skip_gain: float32 [2048], P('ch'), may hold values from -4 to 4
- out_weight: bfloat16 [2048, 8192], P(None, 'ch'), may hold values from -0.125 to 0.125
Outputs:
- output: bfloat16 [8192, 8192], P('ctx', 'ch')
The draws below stay inside these ranges and needn't reach their ends.
All inputs are finite; a program needn't handle non-finite values.
Results may differ from the reference program's by a relative error of at most 0.015.
Values may be sent and summed in bfloat16 or wider, within the bound.
A program may use at most 64 MiB of HBM per device.

```python
import math
import jax
import jax.numpy as jnp
from jax import lax

D = 8192
C = 2048
MODES = 16
LEN = 8192


def levels(key, dims, split, low, top_value):
    def one(position, shards_of):
        steps = jax.random.uniform(jax.random.fold_in(jax.random.fold_in(key, 6), position), (shards_of,), jnp.float32, low / len(split), top_value / len(split))
        return jnp.repeat(jnp.exp(steps), dims[position] // shards_of).reshape((-1,) + (1,) * (len(dims) - position - 1))

    gain = one(*split[0])
    for cut in split[1:]:
        gain = gain * one(*cut)
    return gain


def scatter_about(own_key, dims, width, reach, split=(), held_as=jnp.bfloat16):
    result = width * jax.random.normal(own_key, dims, jnp.float32)
    if split:
        result = result * levels(own_key, dims, split, -0.22, 0.18)
    return jnp.clip(result, -reach, reach).astype(held_as)


def setup_inputs(seed: int = 0) -> dict:
    seeds = jax.random.split(jax.random.key(seed), 9)
    tokens = scatter_about(seeds[0], (LEN, D), 1.0, 6.0, ((0, 64), (1, 4)))
    value_weight = scatter_about(seeds[1], (D, C), D ** -0.5, 0.0625, ((0, 64), (1, 4)))
    gate_stream = scatter_about(seeds[2], (LEN, C), 1.0, 6.0, ((0, 64), (1, 4)))
    decay_rate = jnp.clip(jnp.exp(math.log(800.0) - 7.377759 * jax.random.uniform(seeds[3], (MODES, C), jnp.float32) ** levels(seeds[3], (MODES, C), ((1, 4),), -0.2, 0.2)), 0.5, 800.0)
    frequency = jnp.clip(0.2 * jax.random.uniform(seeds[4], (MODES, C), jnp.float32) ** levels(seeds[4], (MODES, C), ((1, 4),), -0.2, 0.2), 0.0, 0.2)
    residue = scatter_about(seeds[5], (MODES, C), 0.35, 2.5, ((1, 4),), jnp.float32)
    skip_gain = scatter_about(seeds[6], (C,), 1.0, 4.0, ((0, 4),), jnp.float32)
    out_weight = scatter_about(seeds[7], (C, D), C ** -0.5, 0.125, ((1, 4),))
    return dict(tokens=tokens, value_weight=value_weight, gate_stream=gate_stream, decay_rate=decay_rate, frequency=frequency, residue=residue, skip_gain=skip_gain, out_weight=out_weight)


def modal_filter(times, decay_rate, frequency, residue, length):
    mode_rates = decay_rate / length
    mode_amps = residue * jnp.sqrt(2.0 * mode_rates)

    def add_mode(totals, mode_row):
        one_rate, one_freq, one_amp = mode_row
        term = one_amp[None, :] * jnp.exp(-one_rate[None, :] * times[:, None]) * jnp.cos(one_freq[None, :] * times[:, None])
        return (totals + term, None)
    start_total = jnp.zeros((times.shape[0], residue.shape[1]), jnp.float32)
    totals, _ = lax.scan(add_mode, start_total, (mode_rates, frequency, mode_amps))
    return totals

def reference(tokens, value_weight, gate_stream, decay_rate, frequency, residue, skip_gain, out_weight):
    value = jnp.dot(tokens, value_weight, preferred_element_type=jnp.float32).astype(jnp.bfloat16)
    times = jnp.arange(LEN).astype(jnp.float32)
    kernel = modal_filter(times, decay_rate, frequency, residue, LEN)
    spectrum = jnp.fft.rfft(value.astype(jnp.float32), n=2 * LEN, axis=0) * jnp.fft.rfft(kernel, n=2 * LEN, axis=0)
    conv = jnp.fft.irfft(spectrum, n=2 * LEN, axis=0)[:LEN]
    mixed = (gate_stream.astype(jnp.float32) * (conv + skip_gain[None, :] * value.astype(jnp.float32))).astype(jnp.bfloat16)
    return jnp.dot(mixed, out_weight, preferred_element_type=jnp.float32).astype(jnp.bfloat16)
```

```python
import jax
import jax.numpy as jnp
from jax import lax
from jax.experimental import pallas as pl
from jax.experimental.pallas import tpu as pltpu
from jax.sharding import PartitionSpec as P

MESH = pl.DeviceIdType.MESH
F32 = jnp.float32
BF16 = jnp.bfloat16

N = 4
ROWS = 128
FEAT = 2048
CH = 512
LANE = 128
BLOCK = 512
RUN = 32
RUNS = BLOCK // RUN
MODES = 16
SPAN = 8192.0
PIECES = 4
ORDER = (2, 1, 3, 0)


def cmul(ar, ai, br, bi):
    return ar * br - ai * bi, ar * bi + ai * br


def powers(rate, freq, t):
    mag = jnp.exp(-rate * t)
    angle = freq * t
    return mag * jnp.cos(angle), mag * jnp.sin(angle)


def make_tables(par, rate, pre, pim, filt, lev):
    rate[...] = par[0] * (1.0 / SPAN)
    amp = par[2] * jnp.sqrt(2.0 * rate[...])
    first = powers(rate[...], par[1], 1.0)
    lev[0], lev[1] = amp * first[0], amp * first[1]
    lev[2], lev[3] = powers(rate[...], par[1], float(RUN))
    lev[4], lev[5] = powers(rate[...], par[1], float(BLOCK))
    lev[6] = amp
    t = lax.broadcasted_iota(jnp.int32, (RUN, LANE), 0).astype(F32)

    def mode(m, total):
        re, im = powers(rate[pl.ds(m, 1), :], par[1, pl.ds(m, 1), :], t)
        pre[m], pim[m] = re, im
        return total + lev[6, pl.ds(m, 1), :] * re

    filt[...] = lax.fori_loop(0, MODES, mode, jnp.zeros((RUN, LANE), F32))


def run_states(value, runs, pre, pim, sre, sim):
    runs[0:RUN] = jnp.zeros((RUN, RUNS, LANE), F32)

    def split(t, _):
        runs[RUN + t] = value[pl.ds(t, RUNS, stride=RUN), :]
        return 0

    lax.fori_loop(0, RUN, split, 0)

    def modes(pair, _):
        zero = jnp.zeros((RUNS, LANE), F32)
        sums = [zero] * 4
        for t in range(RUN):
            v = runs[RUN + t]
            for i in range(2):
                m = pair * 2 + i
                sums[2 * i] += pre[m, RUN - 1 - t : RUN - t, :] * v
                sums[2 * i + 1] += pim[m, RUN - 1 - t : RUN - t, :] * v
        for i in range(2):
            rows = pl.ds(pl.multiple_of((pair * 2 + i) * RUNS, RUNS), RUNS)
            sre[rows, :] = sums[2 * i]
            sim[rows, :] = sums[2 * i + 1]
        return 0

    lax.fori_loop(0, MODES // 2, modes, 0)


def scan_runs(sre, sim, lev, carry, cre=None, cim=None):
    re, im = carry
    for b in range(RUNS):
        rows = pl.ds(b, MODES, stride=RUNS)
        if cre is not None:
            cre[rows, :], cim[rows, :] = cmul(re, im, lev[0], lev[1])
        re, im = cmul(re, im, lev[2], lev[3])
        re, im = re + sre[rows, :], im + sim[rows, :]
    return re, im


def carry_in(states, lev, block):
    re = im = jnp.zeros((MODES, LANE), F32)
    for other in range(N * N):
        new_re, new_im = cmul(re, im, lev[4], lev[5])
        new_re += states[other, 0:MODES, :].astype(F32)
        new_im += states[other, MODES : 2 * MODES, :].astype(F32)
        re = jnp.where(other < block, new_re, re)
        im = jnp.where(other < block, new_im, im)
    return re, im


def direct(runs, filt, near):
    group = 8
    for start in range(0, RUN, group):

        def lag(step, sums):
            gain = filt[pl.ds(step, 1), :]
            return tuple(
                total + gain * runs[RUN + start + i - step] for i, total in enumerate(sums)
            )

        sums = lax.fori_loop(
            0, start + group, lag, tuple(jnp.zeros((RUNS, LANE), F32) for _ in range(group))
        )
        for i in range(group):
            near[start + i] = sums[i]


def far_part(near, pre, pim, cre, cim, conv):
    group = 4

    def some(step, _):
        start = step * group
        sums = [near[start + i] for i in range(group)]
        for m in range(MODES):
            re = cre[m * RUNS : (m + 1) * RUNS, :]
            im = cim[m * RUNS : (m + 1) * RUNS, :]
            for i in range(group):
                row = pl.ds(start + i, 1)
                sums[i] += pre[m, row, :] * re - pim[m, row, :] * im
        for i in range(group):
            conv[pl.ds(start + i, RUNS, stride=RUN), :] = sums[i]
        return 0

    lax.fori_loop(0, RUN // group, some, 0)


def kernel(
    tokens, weight, gate, decay, freq, residue, skip, out_weight, out,
    tok, wf, gt, par, skip_v, ow, part_out, part_in, value, conv, runs, near, rate, pre, pim, filt, lev,
    sre, sim, cre, cim, states, mixed, seen, acc,
    loc, w1s, w1r, w2s, w2r, gs, gr, tzs, tzr, tcs, tcr, rss, rsr, sts, str_, mxs, mxr,
):
    ctx = lax.axis_index("ctx")
    h = lax.axis_index("ch")
    x, y, q = ctx // 16, (ctx // 4) % 4, ctx % 4
    block = ctx // 4
    across, beside = (q + 2) % 4, q + 1 - 2 * (q % 2)

    def remote(src, dst, ss, rs, where, ch):
        return pltpu.make_async_remote_copy(
            src_ref=src, dst_ref=dst, send_sem=ss, recv_sem=rs, device_id=(where, ch), device_id_type=MESH
        )

    def at(xx, yy, qq):
        return xx * 16 + yy * 4 + qq

    def quarter(i):
        return pl.ds(pl.multiple_of(i * LANE, LANE), LANE)

    sends = []

    def send(*args):
        copy = remote(*args)
        copy.start()
        sends.append(copy)

    def arrive(dst, ss, rs):
        remote(dst, dst, ss, rs, ctx, h).wait_recv()

    itself = (q == x) & (x == h)
    first = []
    for to in range(N):
        src, dst = weight.at[:, to * LANE : (to + 1) * LANE], wf.at[h, y, q]
        copy = remote(src, dst, w1s.at[to], w1r.at[h], at(q, y, to), x)
        mine = itself & (q == to)
        pl.when(jnp.logical_not(mine))(copy.start)
        pl.when(mine)(pltpu.make_async_copy(src, dst, w1r.at[h]).start)
        first.append((mine, copy))

    width = FEAT // PIECES
    for i in range(PIECES):
        cols = pl.ds(i * width, width)
        send(tokens.at[:, cols], tok.at[q, :, cols], tzs.at[i], tzr.at[i], at(x, y, across), h)
    send(tokens, tok.at[q], tcs.at[PIECES], tcr.at[PIECES], at(x, y, beside), h)
    for d in range(1, N):
        to = (q + d) % 4
        send(gate.at[:, quarter(to)], gt.at[q], gs.at[d - 1], gr.at[d - 1], at(x, y, to), h)

    local = [
        (decay.at[:, quarter(q)], par.at[0]),
        (freq.at[:, quarter(q)], par.at[1]),
        (residue.at[:, quarter(q)], par.at[2]),
        (skip.at[:, quarter(q)], skip_v),
        (tokens, tok.at[q]),
        (gate.at[:, quarter(q)], gt.at[q]),
        (out_weight, ow),
    ]
    local = [pltpu.make_async_copy(src, dst, loc.at[i]) for i, (src, dst) in enumerate(local)]
    for copy in local:
        copy.start()

    def ring(chunk, i, stage, d):
        back_x, back_y = (x + 4 - d) % 4, (y + 4 - d) % 4
        if (i + stage) % 2 == 0:
            to = at((x + d) % 4, y, q)
            if stage == 0:
                return wf.at[chunk, y, x], to, wf.at[chunk, y, back_x]
            return wf.at[chunk, :, x], to, wf.at[chunk, :, back_x]
        to = at(x, (y + d) % 4, q)
        if stage == 0:
            return wf.at[chunk, y, x], to, wf.at[chunk, back_y, x]
        return wf.at[chunk, y], to, wf.at[chunk, back_y]

    def spread(chunk, i, stage):
        for d in (2, 1, 3):
            src, to, _ = ring(chunk, i, stage, d)
            send(src, src, w2s.at[i, stage, d - 1], w2r.at[i, stage, d - 1], to, h)

    def spread_end(chunk, i, stage):
        for d in (1, 3, 2):
            _, _, dst = ring(chunk, i, stage, d)
            arrive(dst, w2s.at[i, stage, d - 1], w2r.at[i, stage, d - 1])

    chunks = [(h + d) % 4 for d in ORDER]
    for i, chunk in enumerate(chunks):
        arrive(wf.at[chunk, y, x], w1s.at[0], w1r.at[chunk])
        spread(chunk, i, 0)
    for i, chunk in enumerate(chunks):
        spread_end(chunk, i, 0)
        spread(chunk, i, 1)

    for copy in local[:3]:
        copy.wait()
    make_tables(par, rate, pre, pim, filt, lev)

    for i in range(PIECES):
        piece = tok.at[across, :, pl.ds(i * width, width)]
        arrive(piece, tzs.at[i], tzr.at[i])
        send(piece, piece, tcs.at[i], tcr.at[i], at(x, y, beside), h)
    arrive(tok.at[beside], tcs.at[PIECES], tcr.at[PIECES])
    for i in range(PIECES):
        piece = tok.at[(beside + 2) % 4, :, pl.ds(i * width, width)]
        arrive(piece, tcs.at[i], tcr.at[i])
    for copy in local[3:6]:
        copy.wait()

    for i, (d, chunk) in enumerate(zip(ORDER, chunks)):
        spread_end(chunk, i, 1)

        def rows(j, _):
            total = jnp.dot(
                tok[j], wf[chunk].reshape(FEAT, LANE), preferred_element_type=F32
            )
            here = pl.ds(pl.multiple_of(j * ROWS, ROWS), ROWS)
            if d == 0:
                value[here, :] = total
            else:
                part_out[d - 1, here, :] = total.astype(BF16)
            return 0

        lax.fori_loop(0, N, rows, 0)
        if d != 0:
            send(part_out.at[d - 1], part_in.at[d - 1], rss.at[d - 1], rsr.at[d - 1], ctx, chunk)
    for d in range(1, N):
        arrive(part_in.at[d - 1], rss.at[d - 1], rsr.at[d - 1])
        value[...] += part_in[d - 1].astype(F32)
    value[...] = value[...].astype(BF16).astype(F32)

    run_states(value, runs, pre, pim, sre, sim)
    zero = jnp.zeros((MODES, LANE), F32)
    end_re, end_im = scan_runs(sre, sim, lev, (zero, zero))
    states[block, 0:MODES, :] = end_re.astype(BF16)
    states[block, MODES : 2 * MODES, :] = end_im.astype(BF16)
    for d in range(1, N * N):
        to = (block + d) % 16
        send(states.at[block], states.at[block], sts.at[d - 1], str_.at[d - 1], to * 4 + q, h)
    direct(runs, filt, near)
    for d in range(1, N * N):
        arrive(states.at[(block + 16 - d) % 16], sts.at[d - 1], str_.at[d - 1])
    scan_runs(sre, sim, lev, carry_in(states, lev, block), cre, cim)
    far_part(near, pre, pim, cre, cim, conv)

    for d in range(1, N):
        arrive(gt.at[(q + 4 - d) % 4], gs.at[d - 1], gr.at[d - 1])
    for j in range(N):
        here = pl.ds(j * ROWS, ROWS)
        total = conv[here, :] + skip_v[...] * value[here, :]
        mixed[here, :] = (gt[j].astype(F32) * total).astype(BF16)

    own = None
    for dh in (2, 1, 3, 0):
        for dq in range(N):
            to = (q + dq) % 4
            src = mixed.at[pl.ds(pl.multiple_of(to * ROWS, ROWS), ROWS), :]
            dst = seen.at[h, :, quarter(q)]
            sem = mxs.at[dh * N + dq], mxr.at[dh * N + dq]
            if dh == 0 and dq == 0:
                own = pltpu.make_async_copy(src, dst, sem[1])
                own.start()
            else:
                send(src, dst, *sem, at(x, y, to), (h + dh) % 4)
    local[6].wait()
    for step, dh in enumerate((0, 1, 3, 2)):
        source = (h + 4 - dh) % 4
        for dq in range(N):
            dst = seen.at[source, :, quarter((q + 4 - dq) % 4)]
            if dh == 0 and dq == 0:
                own.wait()
            else:
                arrive(dst, mxs.at[dh * N + dq], mxr.at[dh * N + dq])

        def columns(n, _):
            cols = pl.ds(pl.multiple_of(n * 512, 512), 512)
            deep = pl.ds(pl.multiple_of(source * CH, CH), CH)
            total = jnp.dot(seen[source], ow[deep, cols], preferred_element_type=F32)
            if step > 0:
                total += acc[:, cols]
            if step < N - 1:
                acc[:, cols] = total
            else:
                out[:, cols] = total.astype(BF16)
            return 0

        lax.fori_loop(0, FEAT // 512, columns, 0)

    for copy in sends:
        copy.wait_send()
    for mine, copy in first:
        pl.when(jnp.logical_not(mine))(copy.wait_send)


def on_device(tokens, weight, gate, decay, freq, residue, skip, out_weight):
    vmem, dma = pltpu.VMEM, pltpu.SemaphoreType.DMA
    return pl.pallas_call(
        kernel,
        out_shape=jax.ShapeDtypeStruct((ROWS, FEAT), BF16),
        in_specs=[pl.BlockSpec(memory_space=pl.ANY)] * 8,
        out_specs=pl.BlockSpec(memory_space=pltpu.VMEM),
        scratch_shapes=[
            vmem((N, ROWS, FEAT), BF16),
            vmem((N, N, N, ROWS, LANE), BF16),
            vmem((N, ROWS, LANE), BF16),
            vmem((3, MODES, LANE), F32),
            vmem((1, LANE), F32),
            vmem((N * CH, FEAT), BF16),
            vmem((N - 1, BLOCK, LANE), BF16),
            vmem((N - 1, BLOCK, LANE), BF16),
            vmem((BLOCK, LANE), F32),
            vmem((BLOCK, LANE), F32),
            vmem((2 * RUN, RUNS, LANE), F32),
            vmem((RUN, RUNS, LANE), F32),
            vmem((MODES, LANE), F32),
            vmem((MODES, RUN, LANE), F32),
            vmem((MODES, RUN, LANE), F32),
            vmem((RUN, LANE), F32),
            vmem((7, MODES, LANE), F32),
            vmem((MODES * RUNS, LANE), F32),
            vmem((MODES * RUNS, LANE), F32),
            vmem((MODES * RUNS, LANE), F32),
            vmem((MODES * RUNS, LANE), F32),
            vmem((N * N, 2 * MODES, LANE), BF16),
            vmem((BLOCK, LANE), BF16),
            vmem((N, ROWS, CH), BF16),
            vmem((ROWS, FEAT), F32),
            dma((7,)),
            dma((N,)), dma((N,)),
            dma((N, 2, 3)), dma((N, 2, 3)),
            dma((3,)), dma((3,)),
            dma((PIECES,)), dma((PIECES,)),
            dma((PIECES + 1,)), dma((PIECES + 1,)),
            dma((3,)), dma((3,)),
            dma((15,)), dma((15,)),
            dma((16,)), dma((16,)),
        ],
        compiler_params=pltpu.CompilerParams(
            has_side_effects=True, vmem_limit_bytes=48 * 1024 * 1024
        ),
    )(tokens, weight, gate, decay, freq, residue, skip.reshape(1, CH), out_weight)


def solution(mesh):
    placed = (
        P("ctx", "ch"),
        P("ctx", "ch"),
        P("ctx", "ch"),
        P(None, "ch"),
        P(None, "ch"),
        P(None, "ch"),
        P("ch"),
        P(None, "ch"),
    )
    return jax.shard_map(
        on_device, mesh=mesh, in_specs=placed, out_specs=P("ctx", "ch"), check_vma=False
    )
```

```python
import jax
import jax.numpy as jnp
from jax import lax
from jax.experimental import pallas as pl
from jax.experimental.pallas import tpu as pltpu
from jax.sharding import PartitionSpec as P

MESH = pl.DeviceIdType.MESH
F32 = jnp.float32
BF16 = jnp.bfloat16

N = 4
ROWS = 128
FEAT = 2048
CH = 512
BAND = ROWS // N
LANE = 128
BLOCK = 512
RUN = 32
RUNS = BLOCK // RUN
MODES = 16
SPAN = 8192.0
PIECES = 4
SEMS = 112
ORDER = (2, 1, 3, 0)


def cmul(ar, ai, br, bi):
    return ar * br - ai * bi, ar * bi + ai * br


def powers(rate, freq, t):
    mag = jnp.exp(-rate * t)
    angle = freq * t
    return mag * jnp.cos(angle), mag * jnp.sin(angle)


def make_tables(par, rate, pre, pim, filt, lev):
    rate[...] = par[0] * (1.0 / SPAN)
    amp = par[2] * jnp.sqrt(2.0 * rate[...])
    first = powers(rate[...], par[1], 1.0)
    lev[0], lev[1] = amp * first[0], amp * first[1]
    lev[2], lev[3] = powers(rate[...], par[1], float(RUN))
    lev[4], lev[5] = powers(rate[...], par[1], float(BLOCK))
    lev[6] = amp
    t = lax.broadcasted_iota(jnp.int32, (RUN, LANE), 0).astype(F32)

    def mode(m, total):
        re, im = powers(rate[pl.ds(m, 1), :], par[1, pl.ds(m, 1), :], t)
        pre[m], pim[m] = re, im
        return total + lev[6, pl.ds(m, 1), :] * re

    filt[...] = lax.fori_loop(0, MODES, mode, jnp.zeros((RUN, LANE), F32))


def run_states(value, runs, pre, pim, sre, sim):
    runs[0:RUN] = jnp.zeros((RUN, RUNS, LANE), F32)

    def split(t, _):
        runs[RUN + t] = value[pl.ds(t, RUNS, stride=RUN), :]
        return 0

    lax.fori_loop(0, RUN, split, 0)

    def modes(pair, _):
        zero = jnp.zeros((RUNS, LANE), F32)
        sums = [zero] * 4
        for t in range(RUN):
            v = runs[RUN + t]
            for i in range(2):
                m = pair * 2 + i
                sums[2 * i] += pre[m, RUN - 1 - t : RUN - t, :] * v
                sums[2 * i + 1] += pim[m, RUN - 1 - t : RUN - t, :] * v
        for i in range(2):
            rows = pl.ds(pl.multiple_of((pair * 2 + i) * RUNS, RUNS), RUNS)
            sre[rows, :] = sums[2 * i]
            sim[rows, :] = sums[2 * i + 1]
        return 0

    lax.fori_loop(0, MODES // 2, modes, 0)


def scan_runs(sre, sim, lev, carry, cre=None, cim=None):
    re, im = carry
    for b in range(RUNS):
        rows = pl.ds(b, MODES, stride=RUNS)
        if cre is not None:
            cre[rows, :], cim[rows, :] = cmul(re, im, lev[0], lev[1])
        re, im = cmul(re, im, lev[2], lev[3])
        re, im = re + sre[rows, :], im + sim[rows, :]
    return re, im


def carry_in(states, lev, block):
    re = im = jnp.zeros((MODES, LANE), F32)
    for other in range(N * N):
        new_re, new_im = cmul(re, im, lev[4], lev[5])
        new_re += states[other, 0:MODES, :].astype(F32)
        new_im += states[other, MODES : 2 * MODES, :].astype(F32)
        re = jnp.where(other < block, new_re, re)
        im = jnp.where(other < block, new_im, im)
    return re, im


def direct(runs, filt, near):
    group = 8
    for start in range(0, RUN, group):

        def lag(step, sums):
            gain = filt[pl.ds(step, 1), :]
            return tuple(
                total + gain * runs[RUN + start + i - step] for i, total in enumerate(sums)
            )

        sums = lax.fori_loop(
            0, start + group, lag, tuple(jnp.zeros((RUNS, LANE), F32) for _ in range(group))
        )
        for i in range(group):
            near[start + i] = sums[i]


def far_part(near, pre, pim, cre, cim, conv):
    group = 4

    def some(step, _):
        start = step * group
        sums = [near[start + i] for i in range(group)]
        for m in range(MODES):
            re = cre[m * RUNS : (m + 1) * RUNS, :]
            im = cim[m * RUNS : (m + 1) * RUNS, :]
            for i in range(group):
                row = pl.ds(start + i, 1)
                sums[i] += pre[m, row, :] * re - pim[m, row, :] * im
        for i in range(group):
            conv[pl.ds(start + i, RUNS, stride=RUN), :] = sums[i]
        return 0

    lax.fori_loop(0, RUN // group, some, 0)


def kernel(
    tokens, weight, gate, decay, freq, residue, skip, out_weight, out,
    tok, wf, gt, par, skip_v, ow, part_out, part_in, value, conv, runs, near, rate, pre, pim, filt, lev,
    sre, sim, cre, cim, states, mixed, seen, acc, lifted, loc, sent_sem, got_sem,
):
    ctx = lax.axis_index("ctx")
    h = lax.axis_index("ch")
    x, y, q = ctx // 16, (ctx // 4) % 4, ctx % 4
    block = ctx // 4
    across, beside = (q + 2) % 4, q + 1 - 2 * (q % 2)

    def at(xx, yy, qq):
        return xx * 16 + yy * 4 + qq

    def quarter(i):
        return pl.ds(pl.multiple_of(i * LANE, LANE), LANE)

    def band(i):
        return pl.ds(pl.multiple_of(i * BAND, BAND), BAND)

    names = {}
    sends = []

    def sem(name):
        return names.setdefault(name, len(names))

    def remote(src, dst, out_id, in_id, where, ch):
        return pltpu.make_async_remote_copy(
            src_ref=src, dst_ref=dst, send_sem=sent_sem.at[out_id], recv_sem=got_sem.at[in_id],
            device_id=(where, ch), device_id_type=MESH,
        )

    def send(name, src, dst, where, ch):
        i = sem(name)
        copy = remote(src, dst, i, i, where, ch)
        copy.start()
        sends.append(copy)

    def arrive(name, dst):
        i = sem(name)
        remote(dst, dst, i, i, ctx, h).wait_recv()

    barrier = pltpu.get_barrier_semaphore()

    def greet(where, ch):
        pl.semaphore_signal(barrier, inc=1, device_id=(where, ch), device_id_type=MESH)

    for d in range(1, N * N):
        greet((block + d) % 16 * 4 + q, h)
        greet(at(x, y, (q + d) % 4), (h + d // 4) % 4)
    pl.semaphore_wait(barrier, 2 * (N * N - 1))

    for d in (2, 1, 3):
        to = (x + d) % 4
        send(("lift", d), weight.at[band(to), :], lifted.at[x], at(to, y, q), h)
    keep = pltpu.make_async_copy(weight.at[band(x), :], lifted.at[x], loc.at[8])
    keep.start()

    for d in range(1, N):
        to = (q + d) % 4
        send(("gate", d), gate.at[:, quarter(to)], gt.at[q], at(x, y, to), h)

    local = [
        (decay.at[:, quarter(q)], par.at[0]),
        (freq.at[:, quarter(q)], par.at[1]),
        (residue.at[:, quarter(q)], par.at[2]),
        (skip.at[:, quarter(q)], skip_v),
        (tokens, tok.at[q]),
        (gate.at[:, quarter(q)], gt.at[q]),
        (out_weight, ow),
    ]
    local = [pltpu.make_async_copy(src, dst, loc.at[i]) for i, (src, dst) in enumerate(local)]
    for copy in local:
        copy.start()

    keep.wait()
    for d in (1, 3, 2):
        arrive(("lift", d), lifted.at[(x + 4 - d) % 4])
    keep = []
    for dh in (2, 1, 3, 0):
        for dq in range(N):
            to, ch = (q + dq) % 4, (h + dh) % 4
            src, dst = lifted.at[ch, :, quarter(to)], wf.at[h, y, q, band(x), :]
            if dh == 0 and dq == 0:
                keep.append(pltpu.make_async_copy(src, dst, loc.at[8]))
                keep[0].start()
            else:
                send(("weight", dh, dq), src, dst, at(x, y, to), ch)

    width = FEAT // PIECES
    for i in range(PIECES):
        cols = pl.ds(i * width, width)
        send(("across", i), tokens.at[:, cols], tok.at[q, :, cols], at(x, y, across), h)
    send("beside", tokens, tok.at[q], at(x, y, beside), h)

    def weight_end(d):
        dh = (4 - d) % 4
        for dq in range(N):
            if dh == 0 and dq == 0:
                keep[0].wait()
            else:
                arrive(("weight", dh, dq), wf.at[(h + d) % 4, y, (q + 4 - dq) % 4, band(x), :])

    def ring(chunk, i, stage, d):
        back_x, back_y = (x + 4 - d) % 4, (y + 4 - d) % 4
        along_x, along_y = at((x + d) % 4, y, q), at(x, (y + d) % 4, q)
        if stage == 0:
            src = wf.at[chunk, y, :, band(x), :]
            if i % 2 == 0:
                return src, along_x, wf.at[chunk, y, :, band(back_x), :]
            return src, along_y, wf.at[chunk, back_y, :, band(x), :]
        if i % 2 == 0:
            return wf.at[chunk, y], along_y, wf.at[chunk, back_y]
        return wf.at[chunk, :, :, band(x), :], along_x, wf.at[chunk, :, :, band(back_x), :]

    def spread(chunk, i, stage):
        for d in (2, 1, 3):
            src, to, _ = ring(chunk, i, stage, d)
            send(("spread", i, stage, d), src, src, to, h)

    def spread_end(chunk, i, stage):
        for d in (1, 3, 2):
            arrive(("spread", i, stage, d), ring(chunk, i, stage, d)[2])

    chunks = [(h + d) % 4 for d in ORDER]
    for i, (d, chunk) in enumerate(zip(ORDER, chunks)):
        weight_end(d)
        spread(chunk, i, 0)
    for i, chunk in enumerate(chunks):
        spread_end(chunk, i, 0)
        spread(chunk, i, 1)

    for copy in local[:3]:
        copy.wait()
    make_tables(par, rate, pre, pim, filt, lev)

    for i in range(PIECES):
        piece = tok.at[across, :, pl.ds(i * width, width)]
        arrive(("across", i), piece)
        send(("along", i), piece, piece, at(x, y, beside), h)
    arrive("beside", tok.at[beside])
    for i in range(PIECES):
        arrive(("along", i), tok.at[(beside + 2) % 4, :, pl.ds(i * width, width)])
    for copy in local[3:6]:
        copy.wait()

    for i, (d, chunk) in enumerate(zip(ORDER, chunks)):
        spread_end(chunk, i, 1)

        def rows(j, _):
            total = jnp.dot(
                tok[j], wf[chunk].reshape(FEAT, LANE), preferred_element_type=F32
            )
            here = pl.ds(pl.multiple_of(j * ROWS, ROWS), ROWS)
            if d == 0:
                value[here, :] = total
            else:
                part_out[d - 1, here, :] = total.astype(BF16)
            return 0

        lax.fori_loop(0, N, rows, 0)
        if d != 0:
            send(("sum", d), part_out.at[d - 1], part_in.at[d - 1], ctx, chunk)
    for d in range(1, N):
        arrive(("sum", d), part_in.at[d - 1])
        value[...] += part_in[d - 1].astype(F32)
    value[...] = value[...].astype(BF16).astype(F32)

    run_states(value, runs, pre, pim, sre, sim)
    zero = jnp.zeros((MODES, LANE), F32)
    end_re, end_im = scan_runs(sre, sim, lev, (zero, zero))
    states[block, 0:MODES, :] = end_re.astype(BF16)
    states[block, MODES : 2 * MODES, :] = end_im.astype(BF16)
    for d in range(1, N * N):
        to = (block + d) % 16
        send(("state", d), states.at[block], states.at[block], to * 4 + q, h)
    direct(runs, filt, near)
    for d in range(1, N * N):
        arrive(("state", d), states.at[(block + 16 - d) % 16])
    scan_runs(sre, sim, lev, carry_in(states, lev, block), cre, cim)
    far_part(near, pre, pim, cre, cim, conv)

    for d in range(1, N):
        arrive(("gate", d), gt.at[(q + 4 - d) % 4])
    for j in range(N):
        here = pl.ds(j * ROWS, ROWS)
        total = conv[here, :] + skip_v[...] * value[here, :]
        mixed[here, :] = (gt[j].astype(F32) * total).astype(BF16)

    own = None
    for dh in (2, 1, 3, 0):
        for dq in range(N):
            to = (q + dq) % 4
            src = mixed.at[pl.ds(pl.multiple_of(to * ROWS, ROWS), ROWS), :]
            dst = seen.at[h, :, quarter(q)]
            if dh == 0 and dq == 0:
                own = pltpu.make_async_copy(src, dst, loc.at[7])
                own.start()
            else:
                send(("mixed", dh, dq), src, dst, at(x, y, to), (h + dh) % 4)
    local[6].wait()
    for step, dh in enumerate((0, 1, 3, 2)):
        source = (h + 4 - dh) % 4
        for dq in range(N):
            if dh == 0 and dq == 0:
                own.wait()
            else:
                arrive(("mixed", dh, dq), seen.at[source, :, quarter((q + 4 - dq) % 4)])

        def columns(n, _):
            cols = pl.ds(pl.multiple_of(n * 512, 512), 512)
            deep = pl.ds(pl.multiple_of(source * CH, CH), CH)
            total = jnp.dot(seen[source], ow[deep, cols], preferred_element_type=F32)
            if step > 0:
                total += acc[:, cols]
            if step < N - 1:
                acc[:, cols] = total
            else:
                out[:, cols] = total.astype(BF16)
            return 0

        lax.fori_loop(0, FEAT // 512, columns, 0)

    for copy in sends:
        copy.wait_send()
    assert len(names) <= SEMS


def on_device(tokens, weight, gate, decay, freq, residue, skip, out_weight):
    vmem, dma = pltpu.VMEM, pltpu.SemaphoreType.DMA
    return pl.pallas_call(
        kernel,
        out_shape=jax.ShapeDtypeStruct((ROWS, FEAT), BF16),
        in_specs=[pl.BlockSpec(memory_space=pl.ANY)] * 8,
        out_specs=pl.BlockSpec(memory_space=pltpu.VMEM),
        scratch_shapes=[
            vmem((N, ROWS, FEAT), BF16),
            vmem((N, N, N, ROWS, LANE), BF16),
            vmem((N, ROWS, LANE), BF16),
            vmem((3, MODES, LANE), F32),
            vmem((1, LANE), F32),
            vmem((N * CH, FEAT), BF16),
            vmem((N - 1, BLOCK, LANE), BF16),
            vmem((N - 1, BLOCK, LANE), BF16),
            vmem((BLOCK, LANE), F32),
            vmem((BLOCK, LANE), F32),
            vmem((2 * RUN, RUNS, LANE), F32),
            vmem((RUN, RUNS, LANE), F32),
            vmem((MODES, LANE), F32),
            vmem((MODES, RUN, LANE), F32),
            vmem((MODES, RUN, LANE), F32),
            vmem((RUN, LANE), F32),
            vmem((7, MODES, LANE), F32),
            vmem((MODES * RUNS, LANE), F32),
            vmem((MODES * RUNS, LANE), F32),
            vmem((MODES * RUNS, LANE), F32),
            vmem((MODES * RUNS, LANE), F32),
            vmem((N * N, 2 * MODES, LANE), BF16),
            vmem((BLOCK, LANE), BF16),
            vmem((N, ROWS, CH), BF16),
            vmem((ROWS, FEAT), F32),
            vmem((N, BAND, CH), BF16),
            dma((9,)),
            dma((SEMS,)), dma((SEMS,)),
        ],
        compiler_params=pltpu.CompilerParams(
            collective_id=0, has_side_effects=True, vmem_limit_bytes=60 * 1024 * 1024
        ),
    )(tokens, weight, gate, decay, freq, residue, skip.reshape(1, CH), out_weight)


def solution(mesh):
    placed = (
        P("ctx", "ch"),
        P("ctx", "ch"),
        P("ctx", "ch"),
        P(None, "ch"),
        P(None, "ch"),
        P(None, "ch"),
        P("ch"),
        P(None, "ch"),
    )
    return jax.shard_map(
        on_device, mesh=mesh, in_specs=placed, out_specs=P("ctx", "ch"), check_vma=False
    )
```

```python
import jax
import jax.numpy as jnp
from jax import lax
from jax.experimental import pallas as pl
from jax.experimental.pallas import tpu as pltpu
from jax.sharding import PartitionSpec as P

MESH = pl.DeviceIdType.MESH
F32 = jnp.float32
BF16 = jnp.bfloat16

N = 4
ROWS = 128
FEAT = 2048
CH = 512
BAND = ROWS // N
LANE = 128
BLOCK = 512
RUN = 32
RUNS = BLOCK // RUN
MODES = 16
SPAN = 8192.0
PIECES = 4
SEMS = 160
ORDER = (2, 1, 3, 0)


def cmul(ar, ai, br, bi):
    return ar * br - ai * bi, ar * bi + ai * br


def powers(rate, freq, t):
    mag = jnp.exp(-rate * t)
    angle = freq * t
    return mag * jnp.cos(angle), mag * jnp.sin(angle)


def make_tables(par, rate, pre, pim, filt, lev):
    rate[...] = par[0] * (1.0 / SPAN)
    amp = par[2] * jnp.sqrt(2.0 * rate[...])
    first = powers(rate[...], par[1], 1.0)
    lev[0], lev[1] = amp * first[0], amp * first[1]
    lev[2], lev[3] = powers(rate[...], par[1], float(RUN))
    lev[4], lev[5] = powers(rate[...], par[1], float(BLOCK))
    lev[6] = amp
    t = lax.broadcasted_iota(jnp.int32, (RUN, LANE), 0).astype(F32)

    def mode(m, total):
        re, im = powers(rate[pl.ds(m, 1), :], par[1, pl.ds(m, 1), :], t)
        pre[m], pim[m] = re, im
        return total + lev[6, pl.ds(m, 1), :] * re

    filt[...] = lax.fori_loop(0, MODES, mode, jnp.zeros((RUN, LANE), F32))


def run_states(value, runs, pre, pim, sre, sim):
    runs[0:RUN] = jnp.zeros((RUN, RUNS, LANE), F32)

    def split(t, _):
        runs[RUN + t] = value[pl.ds(t, RUNS, stride=RUN), :]
        return 0

    lax.fori_loop(0, RUN, split, 0)

    def modes(pair, _):
        zero = jnp.zeros((RUNS, LANE), F32)
        sums = [zero] * 4
        for t in range(RUN):
            v = runs[RUN + t]
            for i in range(2):
                m = pair * 2 + i
                sums[2 * i] += pre[m, RUN - 1 - t : RUN - t, :] * v
                sums[2 * i + 1] += pim[m, RUN - 1 - t : RUN - t, :] * v
        for i in range(2):
            rows = pl.ds(pl.multiple_of((pair * 2 + i) * RUNS, RUNS), RUNS)
            sre[rows, :] = sums[2 * i]
            sim[rows, :] = sums[2 * i + 1]
        return 0

    lax.fori_loop(0, MODES // 2, modes, 0)


def scan_runs(sre, sim, lev, carry, cre=None, cim=None):
    re, im = carry
    for b in range(RUNS):
        rows = pl.ds(b, MODES, stride=RUNS)
        if cre is not None:
            cre[rows, :], cim[rows, :] = cmul(re, im, lev[0], lev[1])
        re, im = cmul(re, im, lev[2], lev[3])
        re, im = re + sre[rows, :], im + sim[rows, :]
    return re, im


def carry_in(states, lev, block):
    re = im = jnp.zeros((MODES, LANE), F32)
    for other in range(N * N):
        new_re, new_im = cmul(re, im, lev[4], lev[5])
        new_re += states[other, 0:MODES, :].astype(F32)
        new_im += states[other, MODES : 2 * MODES, :].astype(F32)
        re = jnp.where(other < block, new_re, re)
        im = jnp.where(other < block, new_im, im)
    return re, im


def direct(runs, filt, near):
    group = 8
    for start in range(0, RUN, group):

        def lag(step, sums):
            gain = filt[pl.ds(step, 1), :]
            return tuple(
                total + gain * runs[RUN + start + i - step] for i, total in enumerate(sums)
            )

        sums = lax.fori_loop(
            0, start + group, lag, tuple(jnp.zeros((RUNS, LANE), F32) for _ in range(group))
        )
        for i in range(group):
            near[start + i] = sums[i]


def far_part(near, pre, pim, cre, cim, conv):
    group = 4

    def some(step, _):
        start = step * group
        sums = [near[start + i] for i in range(group)]
        for m in range(MODES):
            re = cre[m * RUNS : (m + 1) * RUNS, :]
            im = cim[m * RUNS : (m + 1) * RUNS, :]
            for i in range(group):
                row = pl.ds(start + i, 1)
                sums[i] += pre[m, row, :] * re - pim[m, row, :] * im
        for i in range(group):
            conv[pl.ds(start + i, RUNS, stride=RUN), :] = sums[i]
        return 0

    lax.fori_loop(0, RUN // group, some, 0)


def kernel(
    tokens, weight, gate, decay, freq, residue, skip, out_weight, out,
    tok, wf, gt, par, skip_v, ow, part_out, part_in, passed, value, conv, runs, near, rate, pre, pim, filt, lev,
    sre, sim, cre, cim, states, mixed, seen, acc, lifted, loc, sent_sem, got_sem,
):
    ctx = lax.axis_index("ctx")
    h = lax.axis_index("ch")
    x, y, q = ctx // 16, (ctx // 4) % 4, ctx % 4
    block = ctx // 4
    across, beside = (q + 2) % 4, q + 1 - 2 * (q % 2)

    def at(xx, yy, qq):
        return xx * 16 + yy * 4 + qq

    def quarter(i):
        return pl.ds(pl.multiple_of(i * LANE, LANE), LANE)

    def band(i):
        return pl.ds(pl.multiple_of(i * BAND, BAND), BAND)

    names = {}
    seen_names = set()
    sends = {}

    def sem(name):
        return names.setdefault(name, len(names))

    def remote(src, dst, out_id, in_id, where, ch):
        return pltpu.make_async_remote_copy(
            src_ref=src, dst_ref=dst, send_sem=sent_sem.at[out_id], recv_sem=got_sem.at[in_id],
            device_id=(where, ch), device_id_type=MESH,
        )

    def send(name, src, dst, where, ch):
        i = sem(name)
        copy = remote(src, dst, i, i, where, ch)
        copy.start()
        sends[name] = copy

    def sent(name):
        sends.pop(name).wait_send()

    def arrive(name, dst):
        if name not in seen_names:
            seen_names.add(name)
            i = sem(name)
            remote(dst, dst, i, i, ctx, h).wait_recv()

    barrier = pltpu.get_barrier_semaphore()

    def greet(where, ch):
        pl.semaphore_signal(barrier, inc=1, device_id=(where, ch), device_id_type=MESH)

    for d in range(1, N * N):
        greet((block + d) % 16 * 4 + q, h)
        greet(at(x, y, (q + d) % 4), (h + d // 4) % 4)
    pl.semaphore_wait(barrier, 2 * (N * N - 1))

    for d in (2, 1, 3):
        to = (x + d) % 4
        send(("lift", d), weight.at[band(to), :], lifted.at[x], at(to, y, q), h)
    keep = pltpu.make_async_copy(weight.at[band(x), :], lifted.at[x], loc.at[8])
    keep.start()

    local = [
        (decay.at[:, quarter(q)], par.at[0]),
        (freq.at[:, quarter(q)], par.at[1]),
        (residue.at[:, quarter(q)], par.at[2]),
        (skip.at[:, quarter(q)], skip_v),
        (tokens, tok.at[q]),
        (gate.at[:, quarter(q)], gt.at[q]),
        (out_weight, ow),
    ]
    local = [pltpu.make_async_copy(src, dst, loc.at[i]) for i, (src, dst) in enumerate(local)]
    for copy in local:
        copy.start()

    base = [sem(("weight", i)) for i in range(N * N)][0]
    last = [sem(("weight sent", i)) for i in range(N * N)][0]
    onward = []
    for d in (0, 1, 3, 2):
        ch = (x + 4 - d) % 4
        if d == 0:
            keep.wait()
        else:
            arrive(("lift", d), lifted.at[ch])
        for dq in range(N):
            to = (q + dq) % 4
            src, dst = lifted.at[ch, :, quarter(to)], wf.at[h, y, q, band(x), :]
            got = base + (ch + 4 - h) % 4 * N + dq
            copy = remote(src, dst, last + d * N + dq, got, at(x, y, to), ch)
            if dq == 0:
                away = ch != h
                pl.when(away)(copy.start)
                pl.when(ch == h)(pltpu.make_async_copy(src, dst, got_sem.at[got]).start)
                onward.append((away, copy))
            else:
                copy.start()
                sends["weight", d, dq] = copy

    width = FEAT // PIECES
    for i in range(PIECES):
        cols = pl.ds(i * width, width)
        send(("across", i), tokens.at[:, cols], tok.at[q, :, cols], at(x, y, across), h)
    send("beside", tokens, tok.at[q], at(x, y, beside), h)

    def weight_end(d):
        for dq in range(N):
            i = base + (4 - d) % 4 * N + dq
            dst = wf.at[(h + d) % 4, y, (q + 4 - dq) % 4, band(x), :]
            remote(dst, dst, i, i, ctx, h).wait_recv()

    def ring(chunk, g, stage, d):
        back_x, back_y = (x + 4 - d) % 4, (y + 4 - d) % 4
        along_x, along_y = at((x + d) % 4, y, q), at(x, (y + d) % 4, q)
        some = pl.ds(2 * g, 2)
        if stage == 0:
            src = wf.at[chunk, y, some, band(x), :]
            if g == 0:
                return src, along_x, wf.at[chunk, y, some, band(back_x), :]
            return src, along_y, wf.at[chunk, back_y, some, band(x), :]
        if g == 0:
            return wf.at[chunk, y, some], along_y, wf.at[chunk, back_y, some]
        return wf.at[chunk, :, some, band(x), :], along_x, wf.at[chunk, :, some, band(back_x), :]

    chunks = [(h + d) % 4 for d in ORDER]
    ways = [(g, d) for d in (2, 1, 3) for g in range(2)]

    def spread(i, stage):
        for g, d in ways:
            src, to, _ = ring(chunks[i], g, stage, d)
            send(("spread", i, g, stage, d), src, src, to, h)

    def spread_end(i, stage):
        for g, d in ways:
            arrive(("spread", i, g, stage, d), ring(chunks[i], g, stage, d)[2])

    def spread_sent(i):
        for g, d in ways:
            sent(("spread", i, g, 1, d))

    def forward(i):
        piece = tok.at[across, :, pl.ds(i * width, width)]
        arrive(("across", i), piece)
        send(("along", i), piece, piece, at(x, y, beside), h)

    for d in (0, 1, 3, 2):
        weight_end(d)
        spread(ORDER.index(d), 0)
    for i in (0, 1):
        spread_end(i, 0)
        spread(i, 1)
    for copy in local[:3]:
        copy.wait()
    make_tables(par, rate, pre, pim, filt, lev)
    forward(0)
    forward(1)
    spread_sent(0)
    spread_end(2, 0)
    spread(2, 1)
    forward(2)
    spread_sent(1)
    spread_end(3, 0)
    spread(3, 1)
    forward(3)
    arrive("beside", tok.at[beside])
    for i in range(PIECES):
        arrive(("along", i), tok.at[(beside + 2) % 4, :, pl.ds(i * width, width)])
    for copy in local[3:6]:
        copy.wait()

    for d in range(1, N):
        to = (q + d) % 4
        send(("gate", d), gate.at[:, quarter(to)], gt.at[q], at(x, y, to), h)

    def product(d):
        i = ORDER.index(d)
        spread_end(i, 1)
        return jnp.dot(
            tok[...].reshape(BLOCK, FEAT), wf[chunks[i]].reshape(FEAT, LANE), preferred_element_type=F32
        )

    half = BLOCK // 2
    low, high = pl.ds(0, half), pl.ds(half, half)

    def give(name, slot, rows, to, ch):
        send(name, part_out.at[slot, rows, :], to, ctx, ch)

    up, down = (h + 1) % 4, (h + 3) % 4
    part_out[2] = product(2).astype(BF16)
    give("hop up", 2, low, passed.at[0], up)
    give("hop down", 2, high, passed.at[1], down)
    total = product(1)
    conv[low, :] = total[:half]
    part_out[0, high, :] = total[half:].astype(BF16)
    give("up high", 0, high, part_in.at[0, high, :], up)
    total = product(3)
    conv[high, :] = total[half:]
    part_out[1, low, :] = total[:half].astype(BF16)
    give("down low", 1, low, part_in.at[1, low, :], down)
    arrive("hop up", passed.at[0])
    part_out[0, low, :] = (conv[low, :] + passed[0].astype(F32)).astype(BF16)
    give("up low", 0, low, part_in.at[0, low, :], up)
    arrive("hop down", passed.at[1])
    part_out[1, high, :] = (conv[high, :] + passed[1].astype(F32)).astype(BF16)
    give("down high", 1, high, part_in.at[1, high, :], down)
    value[...] = product(0)
    arrive("up high", part_in.at[0, high, :])
    arrive("down low", part_in.at[1, low, :])
    arrive("up low", part_in.at[0, low, :])
    arrive("down high", part_in.at[1, high, :])
    value[...] += part_in[0].astype(F32) + part_in[1].astype(F32)
    value[...] = value[...].astype(BF16).astype(F32)

    run_states(value, runs, pre, pim, sre, sim)
    zero = jnp.zeros((MODES, LANE), F32)
    end_re, end_im = scan_runs(sre, sim, lev, (zero, zero))
    states[block, 0:MODES, :] = end_re.astype(BF16)
    states[block, MODES : 2 * MODES, :] = end_im.astype(BF16)
    for d in range(1, N * N):
        to = (block + d) % 16
        send(("state", d), states.at[block], states.at[block], to * 4 + q, h)
    direct(runs, filt, near)
    for d in range(1, N * N):
        arrive(("state", d), states.at[(block + 16 - d) % 16])
    scan_runs(sre, sim, lev, carry_in(states, lev, block), cre, cim)
    far_part(near, pre, pim, cre, cim, conv)

    for d in range(1, N):
        arrive(("gate", d), gt.at[(q + 4 - d) % 4])
    for j in range(N):
        here = pl.ds(j * ROWS, ROWS)
        total = conv[here, :] + skip_v[...] * value[here, :]
        mixed[here, :] = (gt[j].astype(F32) * total).astype(BF16)

    half = ROWS // 2

    def part(i):
        return pl.ds(i * half, half)

    def give_mixed(dh, i):
        for dq in range(N):
            to = (q + dq) % 4
            src = mixed.at[pl.ds(pl.multiple_of(to * ROWS + i * half, half), half), :]
            send(("mixed", dh, i, dq), src, seen.at[h, part(i), quarter(q)], at(x, y, to), (h + dh) % 4)

    def mixed_end(dh, i):
        for dq in range(N):
            dst = seen.at[(h + 4 - dh) % 4, part(i), quarter((q + 4 - dq) % 4)]
            arrive(("mixed", dh, i, dq), dst)

    def whole(to):
        return mixed.at[pl.ds(pl.multiple_of(to * ROWS, ROWS), ROWS), :]

    give_mixed(1, 0)
    give_mixed(3, 1)
    own = pltpu.make_async_copy(whole(q), seen.at[h, :, quarter(q)], loc.at[7])
    own.start()
    for dq in range(N):
        sent(("mixed", 1, 0, dq))
        sent(("mixed", 3, 1, dq))
    for dq in range(1, N):
        to = (q + dq) % 4
        send(("mixed", dq), whole(to), seen.at[h, :, quarter(q)], at(x, y, to), h)
    give_mixed(1, 1)
    give_mixed(3, 0)

    def project(source, step):
        def columns(n, _):
            cols = pl.ds(pl.multiple_of(n * 512, 512), 512)
            deep = pl.ds(pl.multiple_of(source * CH, CH), CH)
            total = jnp.dot(seen[source], ow[deep, cols], preferred_element_type=F32)
            if step > 0:
                total += acc[:, cols]
            if step < N - 1:
                acc[:, cols] = total
            else:
                out[:, cols] = total.astype(BF16)
            return 0

        lax.fori_loop(0, FEAT // 512, columns, 0)

    mixed_end(1, 0)
    src = seen.at[down, part(0), :]
    send("pass up", src, src, ctx, up)
    mixed_end(3, 1)
    src = seen.at[up, part(1), :]
    send("pass down", src, src, ctx, down)
    local[6].wait()
    own.wait()
    for dq in range(1, N):
        arrive(("mixed", dq), seen.at[h, :, quarter((q + 4 - dq) % 4)])
    project(h, 0)
    mixed_end(1, 1)
    project(down, 1)
    mixed_end(3, 0)
    project(up, 2)
    opposite = (h + 2) % 4
    arrive("pass up", seen.at[opposite, part(0), :])
    arrive("pass down", seen.at[opposite, part(1), :])
    project(opposite, 3)

    for copy in sends.values():
        copy.wait_send()
    for away, copy in onward:
        pl.when(away)(copy.wait_send)
    assert len(names) <= SEMS


def on_device(tokens, weight, gate, decay, freq, residue, skip, out_weight):
    vmem, dma = pltpu.VMEM, pltpu.SemaphoreType.DMA
    return pl.pallas_call(
        kernel,
        out_shape=jax.ShapeDtypeStruct((ROWS, FEAT), BF16),
        in_specs=[pl.BlockSpec(memory_space=pl.ANY)] * 8,
        out_specs=pl.BlockSpec(memory_space=pltpu.VMEM),
        scratch_shapes=[
            vmem((N, ROWS, FEAT), BF16),
            vmem((N, N, N, ROWS, LANE), BF16),
            vmem((N, ROWS, LANE), BF16),
            vmem((3, MODES, LANE), F32),
            vmem((1, LANE), F32),
            vmem((N * CH, FEAT), BF16),
            vmem((N - 1, BLOCK, LANE), BF16),
            vmem((2, BLOCK, LANE), BF16),
            vmem((2, BLOCK // 2, LANE), BF16),
            vmem((BLOCK, LANE), F32),
            vmem((BLOCK, LANE), F32),
            vmem((2 * RUN, RUNS, LANE), F32),
            vmem((RUN, RUNS, LANE), F32),
            vmem((MODES, LANE), F32),
            vmem((MODES, RUN, LANE), F32),
            vmem((MODES, RUN, LANE), F32),
            vmem((RUN, LANE), F32),
            vmem((7, MODES, LANE), F32),
            vmem((MODES * RUNS, LANE), F32),
            vmem((MODES * RUNS, LANE), F32),
            vmem((MODES * RUNS, LANE), F32),
            vmem((MODES * RUNS, LANE), F32),
            vmem((N * N, 2 * MODES, LANE), BF16),
            vmem((BLOCK, LANE), BF16),
            vmem((N, ROWS, CH), BF16),
            vmem((ROWS, FEAT), F32),
            vmem((N, BAND, CH), BF16),
            dma((9,)),
            dma((SEMS,)), dma((SEMS,)),
        ],
        compiler_params=pltpu.CompilerParams(
            collective_id=0, has_side_effects=True, vmem_limit_bytes=60 * 1024 * 1024
        ),
    )(tokens, weight, gate, decay, freq, residue, skip.reshape(1, CH), out_weight)


def solution(mesh):
    placed = (
        P("ctx", "ch"),
        P("ctx", "ch"),
        P("ctx", "ch"),
        P(None, "ch"),
        P(None, "ch"),
        P(None, "ch"),
        P("ch"),
        P(None, "ch"),
    )
    return jax.shard_map(
        on_device, mesh=mesh, in_specs=placed, out_specs=P("ctx", "ch"), check_vma=False
    )
```

```python
import jax
import jax.numpy as jnp
from jax import lax
from jax.experimental import pallas as pl
from jax.experimental.pallas import tpu as pltpu
from jax.sharding import PartitionSpec as P

MESH = pl.DeviceIdType.MESH
F32 = jnp.float32
BF16 = jnp.bfloat16

N = 4
ROWS = 128
FEAT = 2048
CH = 512
BAND = ROWS // N
LANE = 128
BLOCK = 512
RUN = 32
RUNS = BLOCK // RUN
HALF = RUNS // 2
MODES = 16
SPAN = 8192.0
PIECES = 4
SEMS = 160
ORDER = (2, 1, 3, 0)


def cmul(ar, ai, br, bi):
    return ar * br - ai * bi, ar * bi + ai * br


def powers(rate, freq, t):
    mag = jnp.exp(-rate * t)
    angle = freq * t
    return mag * jnp.cos(angle), mag * jnp.sin(angle)


def make_tables(par, rate, pre, pim, filt, lev):
    rate[...] = par[0] * (1.0 / SPAN)
    amp = par[2] * jnp.sqrt(2.0 * rate[...])
    first = powers(rate[...], par[1], 1.0)
    lev[0], lev[1] = amp * first[0], amp * first[1]
    lev[2], lev[3] = powers(rate[...], par[1], float(RUN))
    lev[4], lev[5] = powers(rate[...], par[1], float(BLOCK))
    lev[6] = amp
    t = lax.broadcasted_iota(jnp.int32, (RUN, LANE), 0).astype(F32)

    def mode(m, total):
        re, im = powers(rate[pl.ds(m, 1), :], par[1, pl.ds(m, 1), :], t)
        pre[m], pim[m] = re, im
        return total + lev[6, pl.ds(m, 1), :] * re

    filt[...] = lax.fori_loop(0, MODES, mode, jnp.zeros((RUN, LANE), F32))


def run_states(first, value, runs, pre, pim, sre, sim):
    first = pl.multiple_of(first, HALF)
    some = pl.ds(first, HALF)

    def split(t, _):
        runs[t, some, :] = jnp.zeros((HALF, LANE), F32)
        runs[RUN + t, some, :] = value[pl.ds(first * RUN + t, HALF, stride=RUN), :]
        return 0

    lax.fori_loop(0, RUN, split, 0)

    def modes(step, _):
        zero = jnp.zeros((HALF, LANE), F32)
        sums = [zero] * 8
        for t in range(RUN):
            v = runs[RUN + t, some, :]
            for i in range(4):
                m = step * 4 + i
                sums[2 * i] += pre[m, RUN - 1 - t : RUN - t, :] * v
                sums[2 * i + 1] += pim[m, RUN - 1 - t : RUN - t, :] * v
        for i in range(4):
            rows = pl.ds(pl.multiple_of((step * 4 + i) * RUNS + first, HALF), HALF)
            sre[rows, :] = sums[2 * i]
            sim[rows, :] = sums[2 * i + 1]
        return 0

    lax.fori_loop(0, MODES // 4, modes, 0)


def scan_runs(sre, sim, lev, carry, cre=None, cim=None):
    re, im = carry
    for b in range(RUNS):
        rows = pl.ds(b, MODES, stride=RUNS)
        if cre is not None:
            cre[rows, :], cim[rows, :] = cmul(re, im, lev[0], lev[1])
        re, im = cmul(re, im, lev[2], lev[3])
        re, im = re + sre[rows, :], im + sim[rows, :]
    return re, im


def carry_in(states, lev, block):
    re = im = jnp.zeros((MODES, LANE), F32)
    for other in range(N * N):
        new_re, new_im = cmul(re, im, lev[4], lev[5])
        new_re += states[other, 0:MODES, :].astype(F32)
        new_im += states[other, MODES : 2 * MODES, :].astype(F32)
        re = jnp.where(other < block, new_re, re)
        im = jnp.where(other < block, new_im, im)
    return re, im


def direct(runs, filt, near):
    group = 8
    for start in range(0, RUN, group):

        def lag(step, sums):
            gain = filt[pl.ds(step, 1), :]
            return tuple(
                total + gain * runs[RUN + start + i - step] for i, total in enumerate(sums)
            )

        sums = lax.fori_loop(
            0, start + group, lag, tuple(jnp.zeros((RUNS, LANE), F32) for _ in range(group))
        )
        for i in range(group):
            near[start + i] = sums[i]


def far_part(near, pre, pim, cre, cim, conv):
    group = 4

    def some(step, _):
        start = step * group
        sums = [near[start + i] for i in range(group)]
        for m in range(MODES):
            re = cre[m * RUNS : (m + 1) * RUNS, :]
            im = cim[m * RUNS : (m + 1) * RUNS, :]
            for i in range(group):
                row = pl.ds(start + i, 1)
                sums[i] += pre[m, row, :] * re - pim[m, row, :] * im
        for i in range(group):
            conv[pl.ds(start + i, RUNS, stride=RUN), :] = sums[i]
        return 0

    lax.fori_loop(0, RUN // group, some, 0)


def kernel(
    tokens, weight, gate, decay, freq, residue, skip, out_weight, out,
    tok, wf, gt, par, skip_v, ow, part_out, part_in, passed, held, value, conv, runs, near, rate, pre, pim, filt, lev,
    sre, sim, cre, cim, states, mixed, seen, acc, lifted, loc, sent_sem, got_sem,
):
    ctx = lax.axis_index("ctx")
    h = lax.axis_index("ch")
    x, y, q = ctx // 16, (ctx // 4) % 4, ctx % 4
    block = ctx // 4
    across, beside = (q + 2) % 4, q + 1 - 2 * (q % 2)

    def at(xx, yy, qq):
        return xx * 16 + yy * 4 + qq

    def quarter(i):
        return pl.ds(pl.multiple_of(i * LANE, LANE), LANE)

    def band(i):
        return pl.ds(pl.multiple_of(i * BAND, BAND), BAND)

    names = {}
    seen_names = set()
    sends = {}

    def sem(name):
        return names.setdefault(name, len(names))

    def remote(src, dst, out_id, in_id, where, ch):
        return pltpu.make_async_remote_copy(
            src_ref=src, dst_ref=dst, send_sem=sent_sem.at[out_id], recv_sem=got_sem.at[in_id],
            device_id=(where, ch), device_id_type=MESH,
        )

    def send(name, src, dst, where, ch):
        i = sem(name)
        copy = remote(src, dst, i, i, where, ch)
        copy.start()
        sends[name] = copy

    def sent(name):
        sends.pop(name).wait_send()

    def arrive(name, dst):
        if name not in seen_names:
            seen_names.add(name)
            i = sem(name)
            remote(dst, dst, i, i, ctx, h).wait_recv()

    barrier = pltpu.get_barrier_semaphore()

    def greet(where, ch):
        pl.semaphore_signal(barrier, inc=1, device_id=(where, ch), device_id_type=MESH)

    for d in range(1, N * N):
        greet((block + d) % 16 * 4 + q, h)
        greet(at(x, y, (q + d) % 4), (h + d // 4) % 4)
    pl.semaphore_wait(barrier, 2 * (N * N - 1))

    def give_tokens(i):
        rows = pl.ds(i * BAND, BAND)
        send(("across", i), tokens.at[rows, :], tok.at[q, rows, :], at(x, y, across), h)

    for d in (2, 1, 3):
        to = (x + d) % 4
        send(("lift", d), weight.at[band(to), :], lifted.at[x], at(to, y, q), h)
    keep = pltpu.make_async_copy(weight.at[band(x), :], lifted.at[x], loc.at[8])
    keep.start()

    give_tokens(0)
    send("beside", tokens, tok.at[q], at(x, y, beside), h)

    local = [
        (decay.at[:, quarter(q)], par.at[0]),
        (freq.at[:, quarter(q)], par.at[1]),
        (residue.at[:, quarter(q)], par.at[2]),
        (skip.at[:, quarter(q)], skip_v),
        (tokens, tok.at[q]),
        (gate.at[:, quarter(q)], gt.at[q]),
        (out_weight, ow),
    ]
    local = [pltpu.make_async_copy(src, dst, loc.at[i]) for i, (src, dst) in enumerate(local)]
    for copy in local:
        copy.start()

    base = [sem(("weight", i)) for i in range(N * N)][0]
    last = [sem(("weight sent", i)) for i in range(N * N)][0]
    onward = []
    for d in (0, 1, 3, 2):
        ch = (x + 4 - d) % 4
        if d == 0:
            keep.wait()
        else:
            arrive(("lift", d), lifted.at[ch])
        for dq in range(N):
            to = (q + dq) % 4
            src, dst = lifted.at[ch, :, quarter(to)], wf.at[h, y, q, band(x), :]
            got = base + (ch + 4 - h) % 4 * N + dq
            copy = remote(src, dst, last + d * N + dq, got, at(x, y, to), ch)
            if dq == 0:
                away = ch != h
                pl.when(away)(copy.start)
                pl.when(ch == h)(pltpu.make_async_copy(src, dst, got_sem.at[got]).start)
                onward.append((away, copy))
            else:
                copy.start()
                sends["weight", d, dq] = copy

    for i in range(1, PIECES):
        give_tokens(i)

    def weight_end(d):
        for dq in range(N):
            i = base + (4 - d) % 4 * N + dq
            dst = wf.at[(h + d) % 4, y, (q + 4 - dq) % 4, band(x), :]
            remote(dst, dst, i, i, ctx, h).wait_recv()

    def ring(chunk, g, stage, d):
        back_x, back_y = (x + 4 - d) % 4, (y + 4 - d) % 4
        along_x, along_y = at((x + d) % 4, y, q), at(x, (y + d) % 4, q)
        some = pl.ds(2 * g, 2)
        if stage == 0:
            src = wf.at[chunk, y, some, band(x), :]
            if g == 0:
                return src, along_x, wf.at[chunk, y, some, band(back_x), :]
            return src, along_y, wf.at[chunk, back_y, some, band(x), :]
        if g == 0:
            return wf.at[chunk, y, some], along_y, wf.at[chunk, back_y, some]
        return wf.at[chunk, :, some, band(x), :], along_x, wf.at[chunk, :, some, band(back_x), :]

    chunks = [(h + d) % 4 for d in ORDER]

    ways = [(g, d) for d in (2, 1, 3) for g in range(2)]

    def spread(i, stage):
        for g, d in ways:
            src, to, _ = ring(chunks[i], g, stage, d)
            send(("spread", i, g, stage, d), src, src, to, h)

    def spread_end(i, stage):
        for g, d in ways:
            arrive(("spread", i, g, stage, d), ring(chunks[i], g, stage, d)[2])

    def spread_sent(i):
        for g, d in ways:
            sent(("spread", i, g, 1, d))

    def forward(i):
        rows = pl.ds(i * BAND, BAND)
        arrive(("across", i), tok.at[across, rows, :])
        send(("along", i), tok.at[across, rows, :], tok.at[across, rows, :], at(x, y, beside), h)

    up, down = (h + 1) % 4, (h + 3) % 4

    def pair(p):
        return (q // 2 + p) % 2 * 2

    def product(d, p):
        rows = tok[pl.ds(pair(p), 2)].reshape(2 * ROWS, FEAT)
        columns = wf[chunks[ORDER.index(d)]].reshape(FEAT, LANE)
        return jnp.dot(rows, columns, preferred_element_type=F32)

    def give(name, src, dst, ch):
        send(name, src, dst, ctx, ch)

    def far_sums(p):
        a, b = pair(p), pair(p) + 1
        total = product(2, p).astype(BF16)
        part_out[2, a], part_out[2, b] = total[:ROWS], total[ROWS:]
        give(("hop up", p), part_out.at[2, a], passed.at[0, p], up)
        give(("hop down", p), part_out.at[2, b], passed.at[1, p], down)

    def up_sums(p):
        a, b = pair(p), pair(p) + 1
        total = product(1, p)
        held[0, p] = total[:ROWS]
        part_out[0, b] = total[ROWS:].astype(BF16)
        give(("up b", p), part_out.at[0, b], part_in.at[0, b], up)

    def down_sums(p):
        a, b = pair(p), pair(p) + 1
        total = product(3, p)
        held[1, p] = total[ROWS:]
        part_out[1, a] = total[:ROWS].astype(BF16)
        give(("down a", p), part_out.at[1, a], part_in.at[1, a], down)

    def joint_sums(p):
        a, b = pair(p), pair(p) + 1
        arrive(("hop up", p), passed.at[0, p])
        part_out[0, a] = (held[0, p] + passed[0, p].astype(F32)).astype(BF16)
        give(("up a", p), part_out.at[0, a], part_in.at[0, a], up)
        arrive(("hop down", p), passed.at[1, p])
        part_out[1, b] = (held[1, p] + passed[1, p].astype(F32)).astype(BF16)
        give(("down b", p), part_out.at[1, b], part_in.at[1, b], down)

    def own_sums(p):
        value[pl.ds(pl.multiple_of(pair(p) * ROWS, 2 * ROWS), 2 * ROWS), :] = product(0, p)

    def add_sums(p):
        a, b = pair(p), pair(p) + 1
        arrive(("up b", p), part_in.at[0, b])
        arrive(("down a", p), part_in.at[1, a])
        arrive(("up a", p), part_in.at[0, a])
        arrive(("down b", p), part_in.at[1, b])
        for i in (a, b):
            rows = pl.ds(pl.multiple_of(i * ROWS, ROWS), ROWS)
            total = value[rows, :] + (part_in[0, i].astype(F32) + part_in[1, i].astype(F32))
            value[rows, :] = total.astype(BF16).astype(F32)

    for d in (0, 1, 3, 2):
        weight_end(d)
        spread(ORDER.index(d), 0)
    for copy in local[:3]:
        copy.wait()
    make_tables(par, rate, pre, pim, filt, lev)
    for i in range(N):
        spread_end(i, 0)
        spread(i, 1)
    for d in range(1, N):
        to = (q + d) % 4
        send(("gate", d), gate.at[:, quarter(to)], gt.at[q], at(x, y, to), h)
    for i in range(PIECES):
        forward(i)
    for copy in local[3:6]:
        copy.wait()
    arrive("beside", tok.at[beside])
    spread_end(0, 1)
    far_sums(0)
    spread_end(1, 1)
    up_sums(0)
    for i in range(PIECES):
        arrive(("along", i), tok.at[(beside + 2) % 4, pl.ds(i * BAND, BAND), :])
    far_sums(1)
    up_sums(1)
    spread_end(2, 1)
    down_sums(0)
    down_sums(1)
    joint_sums(0)
    joint_sums(1)
    spread_end(3, 1)
    own_sums(0)
    own_sums(1)

    for p in range(2):
        add_sums(p)
        run_states(pair(p) * ROWS // RUN, value, runs, pre, pim, sre, sim)
    zero = jnp.zeros((MODES, LANE), F32)
    end_re, end_im = scan_runs(sre, sim, lev, (zero, zero))
    states[block, 0:MODES, :] = end_re.astype(BF16)
    states[block, MODES : 2 * MODES, :] = end_im.astype(BF16)
    moves = []
    for d in (10, 6, 9, 11, 5, 7, 8, 2, 14, 13, 3, 12, 4, 1, 15):
        i = sem(("state", d))
        there = (block + d) % 16
        out_copy = remote(states.at[block], states.at[block], i, i, there * 4 + q, h)
        back = (block + 16 - d) % 16
        in_copy = remote(states.at[back], states.at[back], i, i, ctx, h)
        after, before = block + d < 16, block >= d
        pl.when(after)(out_copy.start)
        moves.append((after, out_copy, before, in_copy))
    direct(runs, filt, near)
    for after, out_copy, before, in_copy in moves:
        pl.when(before)(in_copy.wait_recv)
        pl.when(after)(out_copy.wait_send)
    scan_runs(sre, sim, lev, carry_in(states, lev, block), cre, cim)
    far_part(near, pre, pim, cre, cim, conv)

    for d in range(1, N):
        arrive(("gate", d), gt.at[(q + 4 - d) % 4])
    for j in range(N):
        here = pl.ds(j * ROWS, ROWS)
        total = conv[here, :] + skip_v[...] * value[here, :]
        mixed[here, :] = (gt[j].astype(F32) * total).astype(BF16)

    half = ROWS // 2

    def part(i):
        return pl.ds(i * half, half)

    def give_mixed(dh, i):
        for dq in range(N):
            to = (q + dq) % 4
            src = mixed.at[pl.ds(pl.multiple_of(to * ROWS + i * half, half), half), :]
            send(("mixed", dh, i, dq), src, seen.at[h, part(i), quarter(q)], at(x, y, to), (h + dh) % 4)

    def mixed_end(dh, i):
        for dq in range(N):
            dst = seen.at[(h + 4 - dh) % 4, part(i), quarter((q + 4 - dq) % 4)]
            arrive(("mixed", dh, i, dq), dst)

    def whole(to):
        return mixed.at[pl.ds(pl.multiple_of(to * ROWS, ROWS), ROWS), :]

    give_mixed(1, 0)
    give_mixed(3, 1)
    own = pltpu.make_async_copy(whole(q), seen.at[h, :, quarter(q)], loc.at[7])
    own.start()
    for dq in range(N):
        sent(("mixed", 1, 0, dq))
        sent(("mixed", 3, 1, dq))
    for dq in range(1, N):
        to = (q + dq) % 4
        send(("mixed", dq), whole(to), seen.at[h, :, quarter(q)], at(x, y, to), h)
    give_mixed(1, 1)
    give_mixed(3, 0)

    def project(source, step):
        def columns(n, _):
            cols = pl.ds(pl.multiple_of(n * 512, 512), 512)
            deep = pl.ds(pl.multiple_of(source * CH, CH), CH)
            total = jnp.dot(seen[source], ow[deep, cols], preferred_element_type=F32)
            if step > 0:
                total += acc[:, cols]
            if step < N - 1:
                acc[:, cols] = total
            else:
                out[:, cols] = total.astype(BF16)
            return 0

        lax.fori_loop(0, FEAT // 512, columns, 0)

    mixed_end(1, 0)
    src = seen.at[down, part(0), :]
    send("pass up", src, src, ctx, up)
    mixed_end(3, 1)
    src = seen.at[up, part(1), :]
    send("pass down", src, src, ctx, down)
    local[6].wait()
    own.wait()
    for dq in range(1, N):
        arrive(("mixed", dq), seen.at[h, :, quarter((q + 4 - dq) % 4)])
    project(h, 0)
    mixed_end(1, 1)
    project(down, 1)
    mixed_end(3, 0)
    project(up, 2)
    opposite = (h + 2) % 4
    arrive("pass up", seen.at[opposite, part(0), :])
    arrive("pass down", seen.at[opposite, part(1), :])
    project(opposite, 3)

    for copy in sends.values():
        copy.wait_send()
    for away, copy in onward:
        pl.when(away)(copy.wait_send)
    assert len(names) <= SEMS


def on_device(tokens, weight, gate, decay, freq, residue, skip, out_weight):
    vmem, dma = pltpu.VMEM, pltpu.SemaphoreType.DMA
    return pl.pallas_call(
        kernel,
        out_shape=jax.ShapeDtypeStruct((ROWS, FEAT), BF16),
        in_specs=[pl.BlockSpec(memory_space=pl.ANY)] * 8,
        out_specs=pl.BlockSpec(memory_space=pltpu.VMEM),
        scratch_shapes=[
            vmem((N, ROWS, FEAT), BF16),
            vmem((N, N, N, ROWS, LANE), BF16),
            vmem((N, ROWS, LANE), BF16),
            vmem((3, MODES, LANE), F32),
            vmem((1, LANE), F32),
            vmem((N * CH, FEAT), BF16),
            vmem((N - 1, N, ROWS, LANE), BF16),
            vmem((2, N, ROWS, LANE), BF16),
            vmem((2, 2, ROWS, LANE), BF16),
            vmem((2, 2, ROWS, LANE), F32),
            vmem((BLOCK, LANE), F32),
            vmem((BLOCK, LANE), F32),
            vmem((2 * RUN, RUNS, LANE), F32),
            vmem((RUN, RUNS, LANE), F32),
            vmem((MODES, LANE), F32),
            vmem((MODES, RUN, LANE), F32),
            vmem((MODES, RUN, LANE), F32),
            vmem((RUN, LANE), F32),
            vmem((7, MODES, LANE), F32),
            vmem((MODES * RUNS, LANE), F32),
            vmem((MODES * RUNS, LANE), F32),
            vmem((MODES * RUNS, LANE), F32),
            vmem((MODES * RUNS, LANE), F32),
            vmem((N * N, 2 * MODES, LANE), BF16),
            vmem((BLOCK, LANE), BF16),
            vmem((N, ROWS, CH), BF16),
            vmem((ROWS, FEAT), F32),
            vmem((N, BAND, CH), BF16),
            dma((9,)),
            dma((SEMS,)), dma((SEMS,)),
        ],
        compiler_params=pltpu.CompilerParams(
            collective_id=0, has_side_effects=True, vmem_limit_bytes=60 * 1024 * 1024
        ),
    )(tokens, weight, gate, decay, freq, residue, skip.reshape(1, CH), out_weight)


def solution(mesh):
    placed = (
        P("ctx", "ch"),
        P("ctx", "ch"),
        P("ctx", "ch"),
        P(None, "ch"),
        P(None, "ch"),
        P(None, "ch"),
        P("ch"),
        P(None, "ch"),
    )
    return jax.shard_map(
        on_device, mesh=mesh, in_specs=placed, out_specs=P("ctx", "ch"), check_vma=False
    )
```

```python
import jax
import jax.numpy as jnp
from jax import lax
from jax.experimental import pallas as pl
from jax.experimental.pallas import tpu as pltpu
from jax.sharding import PartitionSpec as P

MESH = pl.DeviceIdType.MESH
F32 = jnp.float32
BF16 = jnp.bfloat16

N = 4
ROWS = 128
FEAT = 2048
CH = 512
BAND = ROWS // N
LANE = 128
BLOCK = 512
RUN = 32
RUNS = BLOCK // RUN
HALF = RUNS // 2
MODES = 16
SPAN = 8192.0
PIECES = 4
SEMS = 160
ORDER = (2, 1, 3, 0)


def cmul(ar, ai, br, bi):
    return ar * br - ai * bi, ar * bi + ai * br


def powers(rate, freq, t):
    mag = jnp.exp(-rate * t)
    angle = freq * t
    return mag * jnp.cos(angle), mag * jnp.sin(angle)


def make_tables(par, rate, pre, pim, filt, lev):
    rate[...] = par[0] * (1.0 / SPAN)
    amp = par[2] * jnp.sqrt(2.0 * rate[...])
    first = powers(rate[...], par[1], 1.0)
    lev[0], lev[1] = amp * first[0], amp * first[1]
    lev[2], lev[3] = powers(rate[...], par[1], float(RUN))
    lev[4], lev[5] = powers(rate[...], par[1], float(BLOCK))
    lev[6] = amp
    t = lax.broadcasted_iota(jnp.int32, (RUN, LANE), 0).astype(F32)

    def mode(m, total):
        re, im = powers(rate[pl.ds(m, 1), :], par[1, pl.ds(m, 1), :], t)
        pre[m], pim[m] = re, im
        return total + lev[6, pl.ds(m, 1), :] * re

    filt[...] = lax.fori_loop(0, MODES, mode, jnp.zeros((RUN, LANE), F32))


def run_states(first, value, runs, pre, pim, sre, sim):
    first = pl.multiple_of(first, HALF)
    some = pl.ds(first, HALF)

    def split(t, _):
        runs[t, some, :] = jnp.zeros((HALF, LANE), F32)
        runs[RUN + t, some, :] = value[pl.ds(first * RUN + t, HALF, stride=RUN), :]
        return 0

    lax.fori_loop(0, RUN, split, 0)

    def modes(step, _):
        zero = jnp.zeros((HALF, LANE), F32)
        sums = [zero] * 8
        for t in range(RUN):
            v = runs[RUN + t, some, :]
            for i in range(4):
                m = step * 4 + i
                sums[2 * i] += pre[m, RUN - 1 - t : RUN - t, :] * v
                sums[2 * i + 1] += pim[m, RUN - 1 - t : RUN - t, :] * v
        for i in range(4):
            rows = pl.ds(pl.multiple_of((step * 4 + i) * RUNS + first, HALF), HALF)
            sre[rows, :] = sums[2 * i]
            sim[rows, :] = sums[2 * i + 1]
        return 0

    lax.fori_loop(0, MODES // 4, modes, 0)


def scan_runs(sre, sim, lev, carry, cre=None, cim=None):
    re, im = carry
    for b in range(RUNS):
        rows = pl.ds(b, MODES, stride=RUNS)
        if cre is not None:
            cre[rows, :], cim[rows, :] = cmul(re, im, lev[0], lev[1])
        re, im = cmul(re, im, lev[2], lev[3])
        re, im = re + sre[rows, :], im + sim[rows, :]
    return re, im


def carry_in(states, lev, block):
    re = im = jnp.zeros((MODES, LANE), F32)
    for other in range(N * N):
        new_re, new_im = cmul(re, im, lev[4], lev[5])
        new_re += states[other, 0:MODES, :].astype(F32)
        new_im += states[other, MODES : 2 * MODES, :].astype(F32)
        re = jnp.where(other < block, new_re, re)
        im = jnp.where(other < block, new_im, im)
    return re, im


def direct(runs, filt, near):
    group = 8
    for start in range(0, RUN, group):

        def lag(step, sums):
            gain = filt[pl.ds(step, 1), :]
            return tuple(
                total + gain * runs[RUN + start + i - step] for i, total in enumerate(sums)
            )

        sums = lax.fori_loop(
            0, start + group, lag, tuple(jnp.zeros((RUNS, LANE), F32) for _ in range(group))
        )
        for i in range(group):
            near[start + i] = sums[i]


def far_part(near, pre, pim, cre, cim, conv):
    group = 4

    def some(step, _):
        start = step * group
        sums = [near[start + i] for i in range(group)]
        for m in range(MODES):
            re = cre[m * RUNS : (m + 1) * RUNS, :]
            im = cim[m * RUNS : (m + 1) * RUNS, :]
            for i in range(group):
                row = pl.ds(start + i, 1)
                sums[i] += pre[m, row, :] * re - pim[m, row, :] * im
        for i in range(group):
            conv[pl.ds(start + i, RUNS, stride=RUN), :] = sums[i]
        return 0

    lax.fori_loop(0, RUN // group, some, 0)


def kernel(
    tokens, weight, gate, decay, freq, residue, skip, out_weight, out,
    tok, wf, gt, par, skip_v, ow, part_out, part_in, passed, held, value, conv, runs, near, rate, pre, pim, filt, lev,
    sre, sim, cre, cim, states, mixed, seen, acc, lifted, loc, sent_sem, got_sem, ready, done,
):
    ctx = lax.axis_index("ctx")
    h = lax.axis_index("ch")
    x, y, q = ctx // 16, (ctx // 4) % 4, ctx % 4
    block = ctx // 4
    across, beside = (q + 2) % 4, q + 1 - 2 * (q % 2)

    def at(xx, yy, qq):
        return xx * 16 + yy * 4 + qq

    def quarter(i):
        return pl.ds(pl.multiple_of(i * LANE, LANE), LANE)

    def band(i):
        return pl.ds(pl.multiple_of(i * BAND, BAND), BAND)

    names = {}
    seen_names = set()
    sends = {}

    def sem(name):
        return names.setdefault(name, len(names))

    def remote(src, dst, out_id, in_id, where, ch):
        return pltpu.make_async_remote_copy(
            src_ref=src, dst_ref=dst, send_sem=sent_sem.at[out_id], recv_sem=got_sem.at[in_id],
            device_id=(where, ch), device_id_type=MESH,
        )

    def send(name, src, dst, where, ch):
        i = sem(name)
        copy = remote(src, dst, i, i, where, ch)
        copy.start()
        sends[name] = copy

    def sent(name):
        sends.pop(name).wait_send()

    def arrive(name, dst):
        if name not in seen_names:
            seen_names.add(name)
            i = sem(name)
            remote(dst, dst, i, i, ctx, h).wait_recv()

    barrier = pltpu.get_barrier_semaphore()

    def greet(where, ch):
        pl.semaphore_signal(barrier, inc=1, device_id=(where, ch), device_id_type=MESH)

    for d in range(1, N * N):
        greet((block + d) % 16 * 4 + q, h)
        greet(at(x, y, (q + d) % 4), (h + d // 4) % 4)
    pl.semaphore_wait(barrier, 2 * (N * N - 1))

    def give_tokens(i):
        rows = pl.ds(i * BAND, BAND)
        send(("across", i), tokens.at[rows, :], tok.at[q, rows, :], at(x, y, across), h)

    for d in (2, 1, 3):
        to = (x + d) % 4
        send(("lift", d), weight.at[band(to), :], lifted.at[x], at(to, y, q), h)
    keep = pltpu.make_async_copy(weight.at[band(x), :], lifted.at[x], loc.at[8])
    keep.start()

    give_tokens(0)
    send("beside", tokens, tok.at[q], at(x, y, beside), h)

    local = [
        (decay.at[:, quarter(q)], par.at[0]),
        (freq.at[:, quarter(q)], par.at[1]),
        (residue.at[:, quarter(q)], par.at[2]),
        (skip.at[:, quarter(q)], skip_v),
        (tokens, tok.at[q]),
        (gate.at[:, quarter(q)], gt.at[q]),
        (out_weight, ow),
    ]
    local = [pltpu.make_async_copy(src, dst, loc.at[i]) for i, (src, dst) in enumerate(local)]
    for copy in local:
        copy.start()

    base = [sem(("weight", i)) for i in range(N * N)][0]
    last = [sem(("weight sent", i)) for i in range(N * N)][0]
    onward = []
    for d in (0, 1, 3, 2):
        ch = (x + 4 - d) % 4
        if d == 0:
            keep.wait()
        else:
            arrive(("lift", d), lifted.at[ch])
        for dq in range(N):
            to = (q + dq) % 4
            src, dst = lifted.at[ch, :, quarter(to)], wf.at[h, y, q, band(x), :]
            got = base + (ch + 4 - h) % 4 * N + dq
            copy = remote(src, dst, last + d * N + dq, got, at(x, y, to), ch)
            if dq == 0:
                away = ch != h
                pl.when(away)(copy.start)
                pl.when(ch == h)(pltpu.make_async_copy(src, dst, got_sem.at[got]).start)
                onward.append((away, copy))
            else:
                copy.start()
                sends["weight", d, dq] = copy

    for i in range(1, PIECES):
        give_tokens(i)

    def weight_end(d):
        for dq in range(N):
            i = base + (4 - d) % 4 * N + dq
            dst = wf.at[(h + d) % 4, y, (q + 4 - dq) % 4, band(x), :]
            remote(dst, dst, i, i, ctx, h).wait_recv()

    def ring(chunk, g, stage, d):
        back_x, back_y = (x + 4 - d) % 4, (y + 4 - d) % 4
        along_x, along_y = at((x + d) % 4, y, q), at(x, (y + d) % 4, q)
        some = pl.ds(2 * g, 2)
        if stage == 0:
            src = wf.at[chunk, y, some, band(x), :]
            if g == 0:
                return src, along_x, wf.at[chunk, y, some, band(back_x), :]
            return src, along_y, wf.at[chunk, back_y, some, band(x), :]
        if g == 0:
            return wf.at[chunk, y, some], along_y, wf.at[chunk, back_y, some]
        return wf.at[chunk, :, some, band(x), :], along_x, wf.at[chunk, :, some, band(back_x), :]

    chunks = [(h + d) % 4 for d in ORDER]

    ways = [(g, d) for d in (2, 1, 3) for g in range(2)]

    def spread(i, stage):
        for g, d in ways:
            src, to, _ = ring(chunks[i], g, stage, d)
            send(("spread", i, g, stage, d), src, src, to, h)

    def spread_end(i, stage):
        for g, d in ways:
            arrive(("spread", i, g, stage, d), ring(chunks[i], g, stage, d)[2])

    def spread_sent(i):
        for g, d in ways:
            sent(("spread", i, g, 1, d))

    def forward(i):
        rows = pl.ds(i * BAND, BAND)
        arrive(("across", i), tok.at[across, rows, :])
        send(("along", i), tok.at[across, rows, :], tok.at[across, rows, :], at(x, y, beside), h)

    up, down = (h + 1) % 4, (h + 3) % 4

    def pair(p):
        return (q // 2 + p) % 2 * 2

    def product(d, p):
        rows = tok[pl.ds(pair(p), 2)].reshape(2 * ROWS, FEAT)
        columns = wf[chunks[ORDER.index(d)]].reshape(FEAT, LANE)
        return jnp.dot(rows, columns, preferred_element_type=F32)

    def give(name, src, dst, ch):
        send(name, src, dst, ctx, ch)

    def far_sums(p):
        a, b = pair(p), pair(p) + 1
        total = product(2, p).astype(BF16)
        part_out[2, a], part_out[2, b] = total[:ROWS], total[ROWS:]
        give(("hop up", p), part_out.at[2, a], passed.at[0, p], up)
        give(("hop down", p), part_out.at[2, b], passed.at[1, p], down)

    def up_sums(p):
        a, b = pair(p), pair(p) + 1
        total = product(1, p)
        held[0, p] = total[:ROWS]
        part_out[0, b] = total[ROWS:].astype(BF16)
        give(("up b", p), part_out.at[0, b], part_in.at[0, b], up)

    def down_sums(p):
        a, b = pair(p), pair(p) + 1
        total = product(3, p)
        held[1, p] = total[ROWS:]
        part_out[1, a] = total[:ROWS].astype(BF16)
        give(("down a", p), part_out.at[1, a], part_in.at[1, a], down)

    def joint_sums(p):
        a, b = pair(p), pair(p) + 1
        arrive(("hop up", p), passed.at[0, p])
        part_out[0, a] = (held[0, p] + passed[0, p].astype(F32)).astype(BF16)
        give(("up a", p), part_out.at[0, a], part_in.at[0, a], up)
        arrive(("hop down", p), passed.at[1, p])
        part_out[1, b] = (held[1, p] + passed[1, p].astype(F32)).astype(BF16)
        give(("down b", p), part_out.at[1, b], part_in.at[1, b], down)

    def own_sums(p):
        value[pl.ds(pl.multiple_of(pair(p) * ROWS, 2 * ROWS), 2 * ROWS), :] = product(0, p)

    def add_sums(p):
        a, b = pair(p), pair(p) + 1
        arrive(("up b", p), part_in.at[0, b])
        arrive(("down a", p), part_in.at[1, a])
        arrive(("up a", p), part_in.at[0, a])
        arrive(("down b", p), part_in.at[1, b])
        for i in (a, b):
            rows = pl.ds(pl.multiple_of(i * ROWS, ROWS), ROWS)
            total = value[rows, :] + (part_in[0, i].astype(F32) + part_in[1, i].astype(F32))
            value[rows, :] = total.astype(BF16).astype(F32)

    for d in (0, 1, 3, 2):
        weight_end(d)
        spread(ORDER.index(d), 0)
    for copy in local[:3]:
        copy.wait()
    make_tables(par, rate, pre, pim, filt, lev)
    for i in range(N):
        spread_end(i, 0)
        spread(i, 1)
    for d in range(1, N):
        to = (q + d) % 4
        send(("gate", d), gate.at[:, quarter(to)], gt.at[q], at(x, y, to), h)
    for i in range(PIECES):
        forward(i)
    for copy in local[3:6]:
        copy.wait()
    arrive("beside", tok.at[beside])
    spread_end(0, 1)
    far_sums(0)
    spread_end(1, 1)
    up_sums(0)
    for i in range(PIECES):
        arrive(("along", i), tok.at[(beside + 2) % 4, pl.ds(i * BAND, BAND), :])
    far_sums(1)
    up_sums(1)
    spread_end(2, 1)
    down_sums(0)
    down_sums(1)
    joint_sums(0)
    joint_sums(1)
    spread_end(3, 1)
    own_sums(0)
    own_sums(1)

    for p in range(2):
        add_sums(p)
        run_states(pair(p) * ROWS // RUN, value, runs, pre, pim, sre, sim)
    zero = jnp.zeros((MODES, LANE), F32)
    end_re, end_im = scan_runs(sre, sim, lev, (zero, zero))
    states[block, 0:MODES, :] = end_re.astype(BF16)
    states[block, MODES : 2 * MODES, :] = end_im.astype(BF16)
    moves = []
    for d in (10, 6, 9, 11, 5, 7, 8, 2, 14, 13, 3, 12, 4, 1, 15):
        i = sem(("state", d))
        there = (block + d) % 16
        out_copy = remote(states.at[block], states.at[block], i, i, there * 4 + q, h)
        back = (block + 16 - d) % 16
        in_copy = remote(states.at[back], states.at[back], i, i, ctx, h)
        after, before = block + d < 16, block >= d
        pl.when(after)(out_copy.start)
        moves.append((after, out_copy, before, in_copy))
    direct(runs, filt, near)
    for after, out_copy, before, in_copy in moves:
        pl.when(before)(in_copy.wait_recv)
        pl.when(after)(out_copy.wait_send)
    scan_runs(sre, sim, lev, carry_in(states, lev, block), cre, cim)
    far_part(near, pre, pim, cre, cim, conv)

    for d in range(1, N):
        arrive(("gate", d), gt.at[(q + 4 - d) % 4])
    for j in range(N):
        here = pl.ds(j * ROWS, ROWS)
        total = conv[here, :] + skip_v[...] * value[here, :]
        mixed[here, :] = (gt[j].astype(F32) * total).astype(BF16)

    half = ROWS // 2

    def part(i):
        return pl.ds(i * half, half)

    def give_mixed(dh, i):
        for dq in range(N):
            to = (q + dq) % 4
            src = mixed.at[pl.ds(pl.multiple_of(to * ROWS + i * half, half), half), :]
            send(("mixed", dh, i, dq), src, seen.at[h, part(i), quarter(q)], at(x, y, to), (h + dh) % 4)

    def mixed_end(dh, i):
        for dq in range(N):
            dst = seen.at[(h + 4 - dh) % 4, part(i), quarter((q + 4 - dq) % 4)]
            arrive(("mixed", dh, i, dq), dst)

    def whole(to):
        return mixed.at[pl.ds(pl.multiple_of(to * ROWS, ROWS), ROWS), :]

    give_mixed(1, 0)
    give_mixed(3, 1)
    own = pltpu.make_async_copy(whole(q), seen.at[h, :, quarter(q)], loc.at[7])
    own.start()
    for dq in range(N):
        sent(("mixed", 1, 0, dq))
        sent(("mixed", 3, 1, dq))
    for dq in range(1, N):
        to = (q + dq) % 4
        send(("mixed", dq), whole(to), seen.at[h, :, quarter(q)], at(x, y, to), h)
    give_mixed(1, 1)
    give_mixed(3, 0)

    def project(source, step):
        def columns(n, _):
            cols = pl.ds(pl.multiple_of(n * 512, 512), 512)
            deep = pl.ds(pl.multiple_of(source * CH, CH), CH)
            total = jnp.dot(seen[source], ow[deep, cols], preferred_element_type=F32)
            if step > 0:
                total += acc[:, cols]
            if step < N - 1:
                acc[:, cols] = total
            else:
                ready[:, cols] = total.astype(BF16)
                pltpu.make_async_copy(ready.at[:, cols], out.at[:, cols], done.at[n]).start()
            return 0

        lax.fori_loop(0, FEAT // 512, columns, 0)

    mixed_end(1, 0)
    src = seen.at[down, part(0), :]
    send("pass up", src, src, ctx, up)
    mixed_end(3, 1)
    src = seen.at[up, part(1), :]
    send("pass down", src, src, ctx, down)
    local[6].wait()
    own.wait()
    for dq in range(1, N):
        arrive(("mixed", dq), seen.at[h, :, quarter((q + 4 - dq) % 4)])
    project(h, 0)
    mixed_end(1, 1)
    project(down, 1)
    mixed_end(3, 0)
    project(up, 2)
    opposite = (h + 2) % 4
    arrive("pass up", seen.at[opposite, part(0), :])
    arrive("pass down", seen.at[opposite, part(1), :])
    project(opposite, 3)
    for n in range(FEAT // 512):
        cols = pl.ds(n * 512, 512)
        pltpu.make_async_copy(ready.at[:, cols], out.at[:, cols], done.at[n]).wait()

    for copy in sends.values():
        copy.wait_send()
    for away, copy in onward:
        pl.when(away)(copy.wait_send)
    assert len(names) <= SEMS


def on_device(tokens, weight, gate, decay, freq, residue, skip, out_weight):
    vmem, dma = pltpu.VMEM, pltpu.SemaphoreType.DMA
    return pl.pallas_call(
        kernel,
        out_shape=jax.ShapeDtypeStruct((ROWS, FEAT), BF16),
        in_specs=[pl.BlockSpec(memory_space=pl.ANY)] * 8,
        out_specs=pl.BlockSpec(memory_space=pl.ANY),
        scratch_shapes=[
            vmem((N, ROWS, FEAT), BF16),
            vmem((N, N, N, ROWS, LANE), BF16),
            vmem((N, ROWS, LANE), BF16),
            vmem((3, MODES, LANE), F32),
            vmem((1, LANE), F32),
            vmem((N * CH, FEAT), BF16),
            vmem((N - 1, N, ROWS, LANE), BF16),
            vmem((2, N, ROWS, LANE), BF16),
            vmem((2, 2, ROWS, LANE), BF16),
            vmem((2, 2, ROWS, LANE), F32),
            vmem((BLOCK, LANE), F32),
            vmem((BLOCK, LANE), F32),
            vmem((2 * RUN, RUNS, LANE), F32),
            vmem((RUN, RUNS, LANE), F32),
            vmem((MODES, LANE), F32),
            vmem((MODES, RUN, LANE), F32),
            vmem((MODES, RUN, LANE), F32),
            vmem((RUN, LANE), F32),
            vmem((7, MODES, LANE), F32),
            vmem((MODES * RUNS, LANE), F32),
            vmem((MODES * RUNS, LANE), F32),
            vmem((MODES * RUNS, LANE), F32),
            vmem((MODES * RUNS, LANE), F32),
            vmem((N * N, 2 * MODES, LANE), BF16),
            vmem((BLOCK, LANE), BF16),
            vmem((N, ROWS, CH), BF16),
            vmem((ROWS, FEAT), F32),
            vmem((N, BAND, CH), BF16),
            dma((9,)),
            dma((SEMS,)), dma((SEMS,)),
            vmem((ROWS, FEAT), BF16), dma((FEAT // 512,)),
        ],
        compiler_params=pltpu.CompilerParams(
            collective_id=0, has_side_effects=True, vmem_limit_bytes=60 * 1024 * 1024
        ),
    )(tokens, weight, gate, decay, freq, residue, skip.reshape(1, CH), out_weight)


def solution(mesh):
    placed = (
        P("ctx", "ch"),
        P("ctx", "ch"),
        P("ctx", "ch"),
        P(None, "ch"),
        P(None, "ch"),
        P(None, "ch"),
        P("ch"),
        P(None, "ch"),
    )
    return jax.shard_map(
        on_device, mesh=mesh, in_specs=placed, out_specs=P("ctx", "ch"), check_vma=False
    )
```
